512 devices in a mesh: row: 32 (over z, core), col: 16 (over y, x).
Axes of the slice: x: 4, y: 4, z: 16, core: 2. Of those that a mesh axis runs over, the one named last changes fastest.
Arguments:
- slab: float32 [65536, 4096], P('row', 'col'), may hold values from -6 to 6
- panel: float32 [65536, 128], P(('row', 'col')), may hold values from -0.03125 to 0.03125
- tfactor: float32 [128, 128], replicated, as said below
- other_av: float32 [65536, 128], P(('row', 'col')), may hold values from -6 to 6
Outputs:
- updated: float32 [65536, 4096], P('row', 'col')
- correction: float32 [65536, 128], P(('row', 'col'))
The draws below stay inside these ranges and needn't reach their ends.
Inputs may be any that keep to these rules, and one draw needn't show every extreme that they name: `tfactor`: upper triangular.
All inputs are finite; a program needn't handle non-finite values.
Results may differ from the reference program's by a relative error of at most 0.00007.
Values sent between devices are 32-bit elements; how exact they have to be, the bound alone decides.
No kernel may reach another device: no remote copies, remote signals or barrier semaphores. Data moves between devices by JAX's collectives and lax.ppermute only.
A program may use at most 64 MiB of HBM per device.

```python
import jax
import jax.numpy as jnp
from jax import lax

N = 65536
NB = 128
SLAB = 4096


def draw_tfactor(key, part):
    key = jax.random.fold_in(key, 11)
    first, second = jax.random.split(key)
    diag_vals = jax.random.uniform(first, (NB,), jnp.float32, 0.6, 1.4)
    upper = jax.random.normal(second, (NB, NB), jnp.float32) * (0.5 / NB ** 0.5)
    upper = jnp.triu(upper, 1)
    return upper + jnp.diag(diag_vals)


def steps_of(stream_key, extent, cuts, least, largest):
    level, own = 1.0, jax.random.fold_in(stream_key, 6)
    for dim, shards_of in cuts:
        steps = jnp.exp(jax.random.uniform(jax.random.fold_in(own, dim), (shards_of,), jnp.float32, least / len(cuts), largest / len(cuts)))
        level = level * jnp.repeat(steps, extent[dim] // shards_of).reshape([-1 if axis == dim else 1 for axis in range(len(extent))])
    return level


def scatter_about(rng, extent, spread, most, pieces=(), dtype=jnp.bfloat16):
    factor_of = steps_of(rng, extent, pieces, -0.22, 0.18) if pieces else 1.0
    array = jax.random.normal(rng, extent, jnp.float32) * spread * factor_of
    return jnp.minimum(jnp.maximum(array, -most), most).astype(dtype)


def setup_inputs(seed: int = 0) -> dict:
    keys = jax.random.split(jax.random.key(seed), 5)
    slab = scatter_about(keys[0], (N, SLAB), 1.0, 6.0, ((0, 32), (1, 16)), jnp.float32)
    panel = scatter_about(keys[1], (N, NB), (N // 2) ** -0.5, 0.03125, ((0, 512),), jnp.float32)
    tfactor = draw_tfactor(jax.random.fold_in(keys[4], 71), 0)
    other_av = scatter_about(keys[3], (N, NB), 1.0, 6.0, ((0, 512),), jnp.float32)
    return dict(slab=slab, panel=panel, tfactor=tfactor, other_av=other_av)


def reference(slab, panel, tfactor, other_av):
    high = lax.Precision.HIGHEST
    start = N // 2
    cols = slab.shape[1]
    slab_panel = panel[start:start + cols]
    product = other_av + jnp.dot(slab, slab_panel, precision=high, preferred_element_type=jnp.float32)
    wmat = jnp.dot(product, tfactor, precision=high, preferred_element_type=jnp.float32)
    inner = jnp.dot(panel.T, wmat, precision=high, preferred_element_type=jnp.float32)
    shifted = jnp.dot(tfactor.T, inner, precision=high, preferred_element_type=jnp.float32)
    correction = wmat - 0.5 * jnp.dot(panel, shifted, precision=high, preferred_element_type=jnp.float32)
    slab_correction = correction[start:start + cols]
    updated = slab - jnp.dot(panel, slab_correction.T, precision=high, preferred_element_type=jnp.float32)
    updated = updated - jnp.dot(correction, slab_panel.T, precision=high, preferred_element_type=jnp.float32)
    return updated, correction
```

```python
import jax
import jax.numpy as jnp
from jax import lax
from jax.sharding import Mesh, PartitionSpec as P

ROW = ("z", "core")
COL = ("y", "x")
ALL = ROW + COL


def dot(a, b, dims=((1,), (0,))):
    return lax.dot_general(
        a, b, (dims, ((), ())), precision=lax.Precision.HIGHEST, preferred_element_type=jnp.float32
    )


def to_all(value, axis):
    spread = jnp.broadcast_to(value, (lax.axis_size(axis),) + value.shape)
    return lax.all_to_all(spread, axis, 0, 0)


def slab_rows(value):
    nz, ncore, ncol = lax.axis_size("z"), lax.axis_size("core"), lax.axis_size(COL)
    root = nz // 2

    def index(z, core, col):
        return (z * ncore + core) * ncol + col

    held = 0
    for target in (0, nz // 4, nz // 2, 3 * nz // 4):
        pairs = [
            (index(root, k, c), index(target, c % 2, (k * ncol + c) // 2))
            for k in range(ncore)
            for c in range(ncol)
        ]
        held = held + lax.ppermute(value, ALL, pairs)
    step = nz // 8
    while step:
        held = held + lax.ppermute(held, "z", [(z, z + step) for z in range(0, nz, 2 * step)])
        step //= 2
    other = lax.ppermute(held, "core", [(0, 1), (1, 0)])
    first = lax.axis_index("core") == 0
    return jnp.concatenate([jnp.where(first, held, other), jnp.where(first, other, held)], axis=0)


def on_device(slab, panel, tfactor, other_av):
    ncol = lax.axis_size(COL)
    block = panel.shape[0]
    panel_rows = to_all(panel, COL).reshape(ncol * block, -1)
    slab_panel = slab_rows(panel)
    term = dot(slab, slab_panel)
    cross = dot(panel_rows, term, ((0,), (0,))) + dot(panel, other_av, ((0,), (0,)))
    sent = jnp.concatenate(
        [term.reshape(ncol, block, -1), cross.reshape(ncol, block // ncol, -1)], axis=1
    )
    summed = lax.all_to_all(sent, COL, 0, 0).sum(axis=0)
    wmat = dot(summed[:block] + other_av, tfactor)
    wmat_rows = to_all(wmat, COL).reshape(ncol * block, -1)
    slab_wmat = slab_rows(wmat)
    part = summed[block:]
    part = part + lax.ppermute(part, "core", [(0, 1), (1, 0)])
    part = to_all(part, "z").sum(axis=0)
    cross = to_all(part, COL).reshape(block, -1)
    middle = dot(dot(tfactor, cross, ((0,), (0,))), tfactor)
    correction = wmat - 0.5 * dot(panel, middle)
    left = jnp.concatenate([panel_rows, wmat_rows], axis=1)
    right = jnp.concatenate([slab_wmat - 0.5 * dot(slab_panel, middle + middle.T), slab_panel], axis=1)
    updated = slab - dot(left, right, ((1,), (1,)))
    return updated, correction


def solution(mesh):
    nrow, ncol = mesh.devices.shape
    grid = Mesh(mesh.devices.reshape(nrow // 2, 2, 4, ncol // 4), ALL)
    placed = (P(ROW, COL), P(ALL, None), P(), P(ALL, None))
    return jax.shard_map(
        on_device,
        mesh=grid,
        in_specs=placed,
        out_specs=(P(ROW, COL), P(ALL, None)),
        check_vma=False,
    )
```

```python
import jax
import jax.numpy as jnp
from jax import lax
from jax.experimental import pallas as pl
from jax.experimental.pallas import tpu as pltpu
from jax.sharding import Mesh, PartitionSpec as P

ROW = ("z", "core")
COL = ("y", "x")
ALL = ROW + COL
SLICE = 8
VMEM = 24 << 20
F32 = jnp.float32
NN = ((1,), (0,))
NT = ((1,), (1,))
TN = ((0,), (0,))


def exact(a, b, dims=NN):
    return lax.dot_general(
        a, b, (dims, ((), ())), precision=lax.Precision.HIGHEST, preferred_element_type=F32
    )


def split(a):
    high = a.astype(jnp.bfloat16)
    return high, (a - high.astype(F32)).astype(jnp.bfloat16)


def product(a, b, dims):
    def part(p, q):
        return lax.dot_general(p, q, (dims, ((), ())), preferred_element_type=F32)

    return part(a[0], b[0]) + (part(a[0], b[1]) + part(a[1], b[0]))


def copies(value, axis):
    return jnp.broadcast_to(value, (lax.axis_size(axis),) + value.shape)


def to_all(value, axis):
    return lax.all_to_all(copies(value, axis), axis, 0, 0)


def place(value, targets):
    nz, ncore, ncol = lax.axis_size("z"), lax.axis_size("core"), lax.axis_size(COL)

    def index(z, core, col):
        return (z * ncore + core) * ncol + col

    return [
        lax.ppermute(
            value,
            ALL,
            [
                (index(nz // 2, k, c), index(target, c % 2, (k * ncol + c) // 2))
                for k in range(ncore)
                for c in range(ncol)
            ],
        )
        for target in targets
    ]


def send_far(held):
    nz = lax.axis_size("z")
    return [lax.ppermute(held, "z", [(nz // 2, z)]) for z in (nz // 4, 3 * nz // 4, 0)]


def send_near(held):
    nz = lax.axis_size("z")
    step = nz // 8
    while step:
        held = held + lax.ppermute(held, "z", [(z, z + step) for z in range(0, nz, 2 * step)])
        step //= 2
    return held


def swapped(held):
    return lax.ppermute(held, "core", [(0, 1), (1, 0)])


def put_halves(core, mine, other, whole):
    half = mine.shape[0]
    whole[pl.ds(core * half, half), :] = mine[...]
    whole[pl.ds((1 - core) * half, half), :] = other[...]


def first_kernel(core_ref, slab, mine, other, out, whole):
    ncol, block = out.shape[:2]
    block -= SLICE
    put_halves(core_ref[0], mine, other, whole)
    right = split(whole[...])
    for i in range(ncol):
        out[i, :block, :] = product(split(slab[i * block : (i + 1) * block, :]), right, NN)


def cross_kernel(terms, rows, panel, other_av, out):
    ncol, block, nb = rows.shape
    cross = product(split(panel[...]), split(other_av[...]), TN)
    for i in range(ncol):
        cross = cross + product(split(rows[i]), split(terms[i, :block, :]), TN)
    out[:, block:, :] = cross.reshape(ncol, SLICE, nb)


def first(core, slab, rows, panel, other_av, mine, other):
    ncol, block, nb = rows.shape
    vmem = pl.BlockSpec(memory_space=pltpu.VMEM)
    shape = jax.ShapeDtypeStruct((ncol, block + SLICE, nb), F32)
    params = pltpu.CompilerParams(vmem_limit_bytes=VMEM)
    terms = pl.pallas_call(
        first_kernel,
        out_shape=shape,
        in_specs=[pl.BlockSpec(memory_space=pltpu.SMEM)] + [vmem] * 3,
        out_specs=vmem,
        scratch_shapes=[pltpu.VMEM((2 * block, nb), F32)],
        compiler_params=params,
        cost_estimate=pl.CostEstimate(
            flops=6*10**9, bytes_accessed=6 * slab.size, transcendentals=0
        ),
        name="first",
    )(core, slab, mine, other)
    return pl.pallas_call(
        cross_kernel,
        out_shape=shape,
        in_specs=[vmem] * 4,
        out_specs=vmem,
        input_output_aliases={0: 0},
        compiler_params=params,
        cost_estimate=pl.CostEstimate(
            flops=6 * rows.size * nb, bytes_accessed=8 * rows.size, transcendentals=0
        ),
        name="cross",
    )(terms, rows, panel, other_av)


def columns_kernel(core_ref, mine, other, wmine, wother, out):
    core, nb = core_ref[0], mine.shape[1]
    put_halves(core, wmine, wother, out.at[:, :nb])
    put_halves(core, mine, other, out.at[:, nb:])


def columns(core, *halves):
    half, nb = halves[0].shape
    vmem = pl.BlockSpec(memory_space=pltpu.VMEM)
    return pl.pallas_call(
        columns_kernel,
        out_shape=jax.ShapeDtypeStruct((2 * half, 2 * nb), F32),
        in_specs=[pl.BlockSpec(memory_space=pltpu.SMEM)] + [vmem] * 4,
        out_specs=vmem,
        cost_estimate=pl.CostEstimate(flops=6*10**9, bytes_accessed=32 * half * nb, transcendentals=0),
        name="columns",
    )(core, *halves)


def last_kernel(
    slab, rows, found, cross, panel, wmat, tfactor, pair,
    updated, correction, whole, right_high, right_low,
):
    nb = tfactor.shape[0]

    @pl.when(pl.program_id(0) == 0)
    def _():
        inner = exact(cross[...].reshape(nb, nb), tfactor[...])
        middle = exact(tfactor[...], inner, TN)
        correction[...] = wmat[...] - 0.5 * exact(panel[...], middle)
        both = 0.5 * (middle + middle.T)
        whole[...] = pair[...]
        whole[:, :nb] = whole[:, :nb] - exact(whole[:, nb:], both)
        right_high[...], right_low[...] = split(whole[...])

    step, block = found.shape[:2]
    left = jnp.concatenate(
        [rows[...].reshape(step * block, nb), found[...].reshape(step * block, nb)], axis=1
    )
    updated[...] = slab[...] - product(split(left), (right_high[...], right_low[...]), NT)


def last(slab, rows, found, panel, wmat, tfactor, pair):
    ncol, block, nb = rows.shape
    height, width = slab.shape
    step = 4

    def whole(*shape):
        return pl.BlockSpec(shape, lambda i: (0,) * len(shape))

    return pl.pallas_call(
        last_kernel,
        grid=(ncol // step,),
        out_shape=(
            jax.ShapeDtypeStruct(slab.shape, F32),
            jax.ShapeDtypeStruct((block, nb), F32),
        ),
        in_specs=[
            pl.BlockSpec((step * block, width), lambda i: (i, 0)),
            pl.BlockSpec((step, block, nb), lambda i: (i, 0, 0)),
            pl.BlockSpec((step, block, nb), lambda i: (i, 0, 0)),
            pl.BlockSpec((ncol, SLICE, nb), lambda i: (0, block // SLICE, 0)),
        ]
        + [whole(nb, nb)] * 3
        + [whole(width, 2 * nb)],
        out_specs=(pl.BlockSpec((step * block, width), lambda i: (i, 0)), whole(block, nb)),
        scratch_shapes=[
            pltpu.VMEM((width, 2 * nb), F32),
            pltpu.VMEM((width, 2 * nb), jnp.bfloat16),
            pltpu.VMEM((width, 2 * nb), jnp.bfloat16),
        ],
        compiler_params=pltpu.CompilerParams(vmem_limit_bytes=VMEM),
        cost_estimate=pl.CostEstimate(
            flops=12 * slab.size * nb, bytes_accessed=4 * (2 * slab.size + 2 * rows.size), transcendentals=0
        ),
        name="last",
    )(slab, rows, found, found, panel, wmat, tfactor, pair)


def on_device(slab, panel, tfactor, other_av):
    ncol = lax.axis_size(COL)
    block = panel.shape[0]
    core = lax.axis_index("core").astype(jnp.int32)[None]
    spread = copies(panel, COL)
    held = place(panel, (8,))[0]
    held, spread = lax.optimization_barrier((held, spread))
    rows = lax.all_to_all(spread, COL, 0, 0)
    held = held + sum(send_far(held))
    mine = send_near(held)
    other = swapped(mine)
    sent = first(core, slab, rows, panel, other_av, mine, other)
    summed = lax.all_to_all(sent, COL, 0, 0).sum(axis=0)
    wmat = exact(summed[:block] + other_av, tfactor)
    part = summed[block:]
    part = part + swapped(part)
    held = sum(place(wmat, (8, 12, 4, 0)))
    part = to_all(part, "z").sum(axis=0)
    found = to_all(jnp.concatenate([wmat, part], axis=0), COL)
    wmine = send_near(held)
    pair = columns(core, mine, other, wmine, swapped(wmine))
    return last(slab, rows, found, panel, wmat, tfactor, pair)


def solution(mesh):
    nrow, ncol = mesh.devices.shape
    grid = Mesh(mesh.devices.reshape(nrow // 2, 2, 4, ncol // 4), ALL)
    placed = (P(ROW, COL), P(ALL, None), P(), P(ALL, None))
    return jax.shard_map(
        on_device,
        mesh=grid,
        in_specs=placed,
        out_specs=(P(ROW, COL), P(ALL, None)),
        check_vma=False,
    )
```

```python
import jax
import jax.numpy as jnp
from jax import lax
from jax.experimental import pallas as pl
from jax.experimental.pallas import tpu as pltpu
from jax.sharding import Mesh, PartitionSpec as P

ROW = ("z", "core")
COL = ("y", "x")
ALL = ROW + COL
SLICE = 8
VMEM = 16 << 20
PARTS = 4
F32 = jnp.float32
NN = ((1,), (0,))
NT = ((1,), (1,))
TN = ((0,), (0,))


def exact(a, b, dims=NN):
    return lax.dot_general(
        a, b, (dims, ((), ())), precision=lax.Precision.HIGHEST, preferred_element_type=F32
    )


def split(a):
    high = a.astype(jnp.bfloat16)
    return high, (a - high.astype(F32)).astype(jnp.bfloat16)


def product(a, b, dims):
    def part(p, q):
        return lax.dot_general(p, q, (dims, ((), ())), preferred_element_type=F32)

    return part(a[0], b[0]) + (part(a[0], b[1]) + part(a[1], b[0]))


def copies(value, axis):
    return jnp.broadcast_to(value, (lax.axis_size(axis),) + value.shape)


def to_all(value, axis):
    return lax.all_to_all(copies(value, axis), axis, 0, 0)


def place(value, targets):
    nz, ncore, ncol = lax.axis_size("z"), lax.axis_size("core"), lax.axis_size(COL)

    def index(z, core, col):
        return (z * ncore + core) * ncol + col

    return [
        lax.ppermute(
            value,
            ALL,
            [
                (index(nz // 2, k, c), index(target, c % 2, (k * ncol + c) // 2))
                for k in range(ncore)
                for c in range(ncol)
            ],
        )
        for target in targets
    ]


def send_far(held):
    nz = lax.axis_size("z")
    return [lax.ppermute(held, "z", [(nz // 2, z)]) for z in (nz // 4, 3 * nz // 4, 0)]


def send_near(held):
    nz = lax.axis_size("z")
    step = nz // 8
    while step:
        held = held + lax.ppermute(held, "z", [(z, z + step) for z in range(0, nz, 2 * step)])
        step //= 2
    return held


def swapped(held):
    return lax.ppermute(held, "core", [(0, 1), (1, 0)])


def put_halves(core, mine, other, whole):
    half = mine.shape[0]
    whole[pl.ds(core * half, half), :] = mine[...]
    whole[pl.ds((1 - core) * half, half), :] = other[...]


def first_kernel(core_ref, slab, mine, other, out, whole):
    ncol, block = out.shape[:2]
    block -= SLICE
    put_halves(core_ref[0], mine, other, whole)
    right = split(whole[...])
    for i in range(ncol):
        out[i, :block, :] = product(split(slab[i * block : (i + 1) * block, :]), right, NN)


def cross_kernel(terms, rows, panel, other_av, out):
    ncol, block, nb = rows.shape
    cross = product(split(panel[...]), split(other_av[...]), TN)
    for i in range(ncol):
        cross = cross + product(split(rows[i]), split(terms[i, :block, :]), TN)
    out[:, block:, :] = cross.reshape(ncol, SLICE, nb)


def first(core, slab, rows, panel, other_av, mine, other):
    ncol, block, nb = rows.shape
    vmem = pl.BlockSpec(memory_space=pltpu.VMEM)
    shape = jax.ShapeDtypeStruct((ncol, block + SLICE, nb), F32)
    params = pltpu.CompilerParams(vmem_limit_bytes=VMEM)
    terms = pl.pallas_call(
        first_kernel,
        out_shape=shape,
        in_specs=[pl.BlockSpec(memory_space=pltpu.SMEM)] + [vmem] * 3,
        out_specs=vmem,
        scratch_shapes=[pltpu.VMEM((2 * block, nb), F32)],
        compiler_params=params,
        cost_estimate=pl.CostEstimate(
            flops=6*10**9, bytes_accessed=6 * slab.size, transcendentals=0
        ),
        name="first",
    )(core, slab, mine, other)
    return pl.pallas_call(
        cross_kernel,
        out_shape=shape,
        in_specs=[vmem] * 4,
        out_specs=vmem,
        input_output_aliases={0: 0},
        compiler_params=params,
        cost_estimate=pl.CostEstimate(
            flops=6 * rows.size * nb, bytes_accessed=8 * rows.size, transcendentals=0
        ),
        name="cross",
    )(terms, rows, panel, other_av)


def summed_kernel(terms, other_av, tfactor, wmat, part):
    block = wmat.shape[0]
    total = terms[0]
    for i in range(1, terms.shape[0]):
        total = total + terms[i]
    wmat[...] = exact(total[:block] + other_av[...], tfactor[...])
    part[...] = total[block:]


def summed(terms, other_av, tfactor):
    vmem = pl.BlockSpec(memory_space=pltpu.VMEM)
    return pl.pallas_call(
        summed_kernel,
        out_shape=(
            jax.ShapeDtypeStruct(other_av.shape, F32),
            jax.ShapeDtypeStruct((SLICE, other_av.shape[1]), F32),
        ),
        in_specs=[vmem] * 3,
        out_specs=(vmem, vmem),
        compiler_params=pltpu.CompilerParams(vmem_limit_bytes=VMEM),
        cost_estimate=pl.CostEstimate(
            flops=12 * other_av.size * tfactor.shape[0], bytes_accessed=4 * terms.size, transcendentals=0
        ),
        name="summed",
    )(terms, other_av, tfactor)


def relayed_kernel(got, out):
    out[...] = got[...]


def relayed(got):
    vmem = pl.BlockSpec(memory_space=pltpu.VMEM)
    return pl.pallas_call(
        relayed_kernel,
        out_shape=jax.ShapeDtypeStruct(got.shape, F32),
        in_specs=[vmem],
        out_specs=vmem,
        compiler_params=pltpu.CompilerParams(vmem_limit_bytes=VMEM),
        cost_estimate=pl.CostEstimate(flops=60*10**9, bytes_accessed=8 * got.size, transcendentals=0),
        name="relayed",
    )(got)


def columns_kernel(core_ref, mine, other, wmine, wother, out):
    core, nb = core_ref[0], mine.shape[1]
    put_halves(core, wmine, wother, out.at[:, :nb])
    put_halves(core, mine, other, out.at[:, nb:])


def columns(core, *halves):
    half, nb = halves[0].shape
    vmem = pl.BlockSpec(memory_space=pltpu.VMEM)
    return pl.pallas_call(
        columns_kernel,
        out_shape=jax.ShapeDtypeStruct((2 * half, 2 * nb), F32),
        in_specs=[pl.BlockSpec(memory_space=pltpu.SMEM)] + [vmem] * 4,
        out_specs=vmem,
        compiler_params=pltpu.CompilerParams(vmem_limit_bytes=VMEM),
        cost_estimate=pl.CostEstimate(flops=6*10**9, bytes_accessed=32 * half * nb, transcendentals=0),
        name="columns",
    )(core, *halves)


def last_kernel(
    slab, rows, found, panel, wmat, tfactor, pair, updated, correction, result, sems
):
    ncol, block, nb = rows.shape
    factor = split(tfactor[...])
    inner = product(split(found[:, block:, :].reshape(nb, nb)), factor, NN)
    middle = product(factor, split(inner), TN)
    both = 0.5 * (middle + middle.T)
    right = pair[...]
    columns_v = right[:, nb:]
    turned = right[:, :nb] - product(split(columns_v), split(both), NN)
    right = split(jnp.concatenate([turned, columns_v], axis=1))
    size = slab.shape[0] // PARTS
    step = ncol // PARTS
    stores = []
    for i in range(PARTS):
        here, part = pl.ds(i * size, size), slice(i * step, (i + 1) * step)
        left = jnp.concatenate(
            [rows[part].reshape(size, nb), found[part, :block, :].reshape(size, nb)], axis=1
        )
        result[here, :] = slab[here, :] - product(split(left), right, NT)
        stores.append(pltpu.make_async_copy(result.at[here, :], updated.at[here, :], sems.at[i]))
        stores[-1].start()
    correction[...] = wmat[...] - 0.5 * product(split(panel[...]), split(middle), NN)
    for store in stores:
        store.wait()


def last(slab, rows, found, panel, wmat, tfactor, pair):
    vmem = pl.BlockSpec(memory_space=pltpu.VMEM)
    return pl.pallas_call(
        last_kernel,
        out_shape=(
            jax.ShapeDtypeStruct(slab.shape, F32),
            jax.ShapeDtypeStruct(wmat.shape, F32),
        ),
        in_specs=[vmem] * 7,
        out_specs=(pl.BlockSpec(memory_space=pl.ANY), vmem),
        scratch_shapes=[pltpu.VMEM(slab.shape, F32), pltpu.SemaphoreType.DMA((PARTS,))],
        compiler_params=pltpu.CompilerParams(vmem_limit_bytes=VMEM),
        cost_estimate=pl.CostEstimate(
            flops=12 * slab.size * wmat.shape[1],
            bytes_accessed=4 * (2 * slab.size + 2 * rows.size),
            transcendentals=0,
        ),
        name="last",
    )(slab, rows, found, panel, wmat, tfactor, pair)


def on_device(slab, panel, tfactor, other_av):
    ncol = lax.axis_size(COL)
    block = panel.shape[0]
    core = lax.axis_index("core").astype(jnp.int32)[None]
    tied, spread = lax.optimization_barrier((panel, copies(panel, COL)))
    rows = lax.all_to_all(spread, COL, 0, 0)
    held = sum(place(tied, (8, 12, 4, 0)))
    mine = send_near(held)
    other = swapped(mine)
    sent = first(core, slab, rows, panel, other_av, mine, other)
    wmat, part = summed(lax.all_to_all(sent, COL, 0, 0), other_av, tfactor)
    part = part + swapped(part)
    early = relayed(sum(place(wmat, (12, 4, 0))))
    held = early + place(wmat, (8,))[0]
    part = lax.all_to_all(
        copies(part, "z"), "z", 0, 0, axis_index_groups=[[(i + 8) % 16 for i in range(16)]]
    ).sum(axis=0)
    found = to_all(jnp.concatenate([wmat, part], axis=0), COL)
    wmine = send_near(held)
    pair = columns(core, mine, other, wmine, swapped(wmine))
    return last(slab, rows, found, panel, wmat, tfactor, pair)


def solution(mesh):
    nrow, ncol = mesh.devices.shape
    grid = Mesh(mesh.devices.reshape(nrow // 2, 2, 4, ncol // 4), ALL)
    placed = (P(ROW, COL), P(ALL, None), P(), P(ALL, None))
    return jax.shard_map(
        on_device,
        mesh=grid,
        in_specs=placed,
        out_specs=(P(ROW, COL), P(ALL, None)),
        check_vma=False,
    )
```

```python
import jax
import jax.numpy as jnp
from jax import lax
from jax.experimental import pallas as pl
from jax.experimental.pallas import tpu as pltpu
from jax.sharding import Mesh, PartitionSpec as P

ROW = ("z", "core")
COL = ("y", "x")
ALL = ROW + COL
SLICE = 8
VMEM = 16 << 20
LAST_VMEM = 50 << 20
PARTS = 2
F32 = jnp.float32
NN = ((1,), (0,))
NT = ((1,), (1,))
TN = ((0,), (0,))


def exact(a, b, dims=NN):
    return lax.dot_general(
        a, b, (dims, ((), ())), precision=lax.Precision.HIGHEST, preferred_element_type=F32
    )


def split(a):
    high = a.astype(jnp.bfloat16)
    return high, (a - high.astype(F32)).astype(jnp.bfloat16)


def product(a, b, dims):
    def part(p, q):
        return lax.dot_general(p, q, (dims, ((), ())), preferred_element_type=F32)

    return part(a[0], b[0]) + (part(a[0], b[1]) + part(a[1], b[0]))


def copies(value, axis):
    return jnp.broadcast_to(value, (lax.axis_size(axis),) + value.shape)


def to_all(value, axis):
    return lax.all_to_all(copies(value, axis), axis, 0, 0)


def place(value, targets):
    nz, ncore, ncol = lax.axis_size("z"), lax.axis_size("core"), lax.axis_size(COL)

    def index(z, core, col):
        return (z * ncore + core) * ncol + col

    return [
        lax.ppermute(
            value,
            ALL,
            [
                (index(nz // 2, k, c), index(target, c % 2, (k * ncol + c) // 2))
                for k in range(ncore)
                for c in range(ncol)
            ],
        )
        for target in targets
    ]


def send_far(held):
    nz = lax.axis_size("z")
    return [lax.ppermute(held, "z", [(nz // 2, z)]) for z in (nz // 4, 3 * nz // 4, 0)]


def send_near(held):
    nz = lax.axis_size("z")
    step = nz // 8
    while step:
        held = held + lax.ppermute(held, "z", [(z, z + step) for z in range(0, nz, 2 * step)])
        step //= 2
    return held


def swapped(held):
    return lax.ppermute(held, "core", [(0, 1), (1, 0)])


def put_halves(core, mine, other, whole):
    half = mine.shape[0]
    whole[pl.ds(core * half, half), :] = mine[...]
    whole[pl.ds((1 - core) * half, half), :] = other[...]


def first_kernel(core_ref, slab, mine, other, out, whole):
    ncol, block = out.shape[:2]
    block -= SLICE
    put_halves(core_ref[0], mine, other, whole)
    right = split(whole[...])
    for i in range(ncol):
        out[i, :block, :] = product(split(slab[i * block : (i + 1) * block, :]), right, NN)


def cross_kernel(terms, rows, panel, other_av, out):
    ncol, block, nb = rows.shape
    cross = product(split(panel[...]), split(other_av[...]), TN)
    for i in range(ncol):
        cross = cross + product(split(rows[i]), split(terms[i, :block, :]), TN)
    out[:, block:, :] = cross.reshape(ncol, SLICE, nb)


def first(core, slab, rows, panel, other_av, mine, other):
    ncol, block, nb = rows.shape
    vmem = pl.BlockSpec(memory_space=pltpu.VMEM)
    shape = jax.ShapeDtypeStruct((ncol, block + SLICE, nb), F32)
    params = pltpu.CompilerParams(vmem_limit_bytes=VMEM)
    terms = pl.pallas_call(
        first_kernel,
        out_shape=shape,
        in_specs=[pl.BlockSpec(memory_space=pltpu.SMEM)] + [vmem] * 3,
        out_specs=vmem,
        scratch_shapes=[pltpu.VMEM((2 * block, nb), F32)],
        compiler_params=params,
        cost_estimate=pl.CostEstimate(
            flops=6*10**9, bytes_accessed=6 * slab.size, transcendentals=0
        ),
        name="first",
    )(core, slab, mine, other)
    return pl.pallas_call(
        cross_kernel,
        out_shape=shape,
        in_specs=[vmem] * 4,
        out_specs=vmem,
        input_output_aliases={0: 0},
        compiler_params=params,
        cost_estimate=pl.CostEstimate(
            flops=6 * rows.size * nb, bytes_accessed=8 * rows.size, transcendentals=0
        ),
        name="cross",
    )(terms, rows, panel, other_av)


def summed_kernel(terms, other_av, tfactor, wmat, part):
    block = wmat.shape[0]
    total = terms[0]
    for i in range(1, terms.shape[0]):
        total = total + terms[i]
    wmat[...] = exact(total[:block] + other_av[...], tfactor[...])
    part[...] = total[block:]


def summed(terms, other_av, tfactor):
    vmem = pl.BlockSpec(memory_space=pltpu.VMEM)
    return pl.pallas_call(
        summed_kernel,
        out_shape=(
            jax.ShapeDtypeStruct(other_av.shape, F32),
            jax.ShapeDtypeStruct((SLICE, other_av.shape[1]), F32),
        ),
        in_specs=[vmem] * 3,
        out_specs=(vmem, vmem),
        compiler_params=pltpu.CompilerParams(vmem_limit_bytes=VMEM),
        cost_estimate=pl.CostEstimate(
            flops=12 * other_av.size * tfactor.shape[0], bytes_accessed=4 * terms.size, transcendentals=0
        ),
        name="summed",
    )(terms, other_av, tfactor)


def spread_kernel(part, other, out):
    total = part[...] + other[...]
    for i in range(out.shape[0]):
        out[i] = total


def spread_sum(part, other):
    vmem = pl.BlockSpec(memory_space=pltpu.VMEM)
    return pl.pallas_call(
        spread_kernel,
        out_shape=jax.ShapeDtypeStruct((lax.axis_size("z"),) + part.shape, F32),
        in_specs=[vmem] * 2,
        out_specs=vmem,
        compiler_params=pltpu.CompilerParams(vmem_limit_bytes=VMEM),
        cost_estimate=pl.CostEstimate(flops=1*10**9, bytes_accessed=128 * part.size, transcendentals=0),
        name="spread",
    )(part, other)


def relayed_kernel(got, out):
    out[...] = got[...]


def relayed(got):
    vmem = pl.BlockSpec(memory_space=pltpu.VMEM)
    return pl.pallas_call(
        relayed_kernel,
        out_shape=jax.ShapeDtypeStruct(got.shape, F32),
        in_specs=[vmem],
        out_specs=vmem,
        compiler_params=pltpu.CompilerParams(vmem_limit_bytes=VMEM),
        cost_estimate=pl.CostEstimate(flops=60*10**9, bytes_accessed=8 * got.size, transcendentals=0),
        name="relayed",
    )(got)


def columns_kernel(core_ref, mine, other, wmine, wother, out):
    core, nb = core_ref[0], mine.shape[1]
    put_halves(core, wmine, wother, out.at[:, :nb])
    put_halves(core, mine, other, out.at[:, nb:])


def columns(core, *halves):
    half, nb = halves[0].shape
    vmem = pl.BlockSpec(memory_space=pltpu.VMEM)
    return pl.pallas_call(
        columns_kernel,
        out_shape=jax.ShapeDtypeStruct((2 * half, 2 * nb), F32),
        in_specs=[pl.BlockSpec(memory_space=pltpu.SMEM)] + [vmem] * 4,
        out_specs=vmem,
        compiler_params=pltpu.CompilerParams(vmem_limit_bytes=VMEM),
        cost_estimate=pl.CostEstimate(flops=6*10**9, bytes_accessed=32 * half * nb, transcendentals=0),
        name="columns",
    )(core, *halves)


def last_kernel(
    slab, rows, found, panel, wmat, tfactor, pair, updated, correction, result, loads, sems
):
    ncol, block, nb = rows.shape
    size = slab.shape[0] // PARTS
    copies = []
    for i in range(PARTS):
        here = pl.ds(i * size, size)
        copies.append(pltpu.make_async_copy(slab.at[here, :], result.at[here, :], loads.at[i]))
        copies[-1].start()
    factor = split(tfactor[...])
    inner = product(split(found[:, block:, :].reshape(nb, nb)), factor, NN)
    middle = product(factor, split(inner), TN)
    both = 0.5 * (middle + middle.T)
    right = pair[...]
    columns_v = right[:, nb:]
    turned = right[:, :nb] - product(split(columns_v), split(both), NN)
    right = split(jnp.concatenate([turned, columns_v], axis=1))
    step = ncol // PARTS
    stores = []
    for i in range(PARTS):
        here, part = pl.ds(i * size, size), slice(i * step, (i + 1) * step)
        left = jnp.concatenate(
            [rows[part].reshape(size, nb), found[part, :block, :].reshape(size, nb)], axis=1
        )
        change = product(split(left), right, NT)
        copies[i].wait()
        result[here, :] = result[here, :] - change
        stores.append(pltpu.make_async_copy(result.at[here, :], updated.at[here, :], sems.at[i]))
        stores[-1].start()
    correction[...] = wmat[...] - 0.5 * product(split(panel[...]), split(middle), NN)
    for store in stores:
        store.wait()


def last(slab, rows, found, panel, wmat, tfactor, pair):
    vmem = pl.BlockSpec(memory_space=pltpu.VMEM)
    return pl.pallas_call(
        last_kernel,
        out_shape=(
            jax.ShapeDtypeStruct(slab.shape, F32),
            jax.ShapeDtypeStruct(wmat.shape, F32),
        ),
        in_specs=[pl.BlockSpec(memory_space=pl.ANY)] + [vmem] * 6,
        out_specs=(pl.BlockSpec(memory_space=pl.ANY), vmem),
        scratch_shapes=[pltpu.VMEM(slab.shape, F32)] + [pltpu.SemaphoreType.DMA((PARTS,))] * 2,
        compiler_params=pltpu.CompilerParams(vmem_limit_bytes=LAST_VMEM),
        cost_estimate=pl.CostEstimate(
            flops=12 * slab.size * wmat.shape[1],
            bytes_accessed=4 * (2 * slab.size + 2 * rows.size),
            transcendentals=0,
        ),
        name="last",
    )(slab, rows, found, panel, wmat, tfactor, pair)


def on_device(slab, panel, tfactor, other_av):
    ncol = lax.axis_size(COL)
    block = panel.shape[0]
    core = lax.axis_index("core").astype(jnp.int32)[None]
    tied, spread = lax.optimization_barrier((panel, copies(panel, COL)))
    rows = lax.all_to_all(spread, COL, 0, 0)
    held = sum(place(tied, (8, 12, 4, 0)))
    mine = send_near(held)
    other = swapped(mine)
    sent = first(core, slab, rows, panel, other_av, mine, other)
    wmat, part = summed(lax.all_to_all(sent, COL, 0, 0), other_av, tfactor)
    other_part = swapped(part)
    early = relayed(sum(place(wmat, (12, 4, 0))))
    held = early + place(wmat, (8,))[0]
    part = lax.all_to_all(
        spread_sum(part, other_part), "z", 0, 0, axis_index_groups=[[(i + 8) % 16 for i in range(16)]]
    ).sum(axis=0)
    found = to_all(jnp.concatenate([wmat, part], axis=0), COL)
    wmine = send_near(held)
    pair = columns(core, mine, other, wmine, swapped(wmine))
    return last(slab, rows, found, panel, wmat, tfactor, pair)


def solution(mesh):
    nrow, ncol = mesh.devices.shape
    grid = Mesh(mesh.devices.reshape(nrow // 2, 2, 4, ncol // 4), ALL)
    placed = (P(ROW, COL), P(ALL, None), P(), P(ALL, None))
    return jax.shard_map(
        on_device,
        mesh=grid,
        in_specs=placed,
        out_specs=(P(ROW, COL), P(ALL, None)),
        check_vma=False,
    )
```

```python
import jax
import jax.numpy as jnp
from jax import lax
from jax.experimental import pallas as pl
from jax.experimental.pallas import tpu as pltpu
from jax.sharding import Mesh, PartitionSpec as P

ROW = ("z", "core")
COL = ("y", "x")
ALL = ROW + COL
SLICE = 8
VMEM = 16 << 20
LAST_VMEM = 50 << 20
PARTS = 2
F32 = jnp.float32
NN = ((1,), (0,))
NT = ((1,), (1,))
TN = ((0,), (0,))


def exact(a, b, dims=NN):
    return lax.dot_general(
        a, b, (dims, ((), ())), precision=lax.Precision.HIGHEST, preferred_element_type=F32
    )


def split(a):
    high = a.astype(jnp.bfloat16)
    return high, (a - high.astype(F32)).astype(jnp.bfloat16)


def product(a, b, dims):
    def part(p, q):
        return lax.dot_general(p, q, (dims, ((), ())), preferred_element_type=F32)

    return part(a[0], b[0]) + (part(a[0], b[1]) + part(a[1], b[0]))


def copies(value, axis):
    return jnp.broadcast_to(value, (lax.axis_size(axis),) + value.shape)


def to_all(value, axis):
    return lax.all_to_all(copies(value, axis), axis, 0, 0)


def place(value, targets):
    nz, ncore, ncol = lax.axis_size("z"), lax.axis_size("core"), lax.axis_size(COL)

    def index(z, core, col):
        return (z * ncore + core) * ncol + col

    return [
        lax.ppermute(
            value,
            ALL,
            [
                (index(nz // 2, k, c), index(target, c % 2, (k * ncol + c) // 2))
                for k in range(ncore)
                for c in range(ncol)
            ],
        )
        for target in targets
    ]


def send_far(held):
    nz = lax.axis_size("z")
    return [lax.ppermute(held, "z", [(nz // 2, z)]) for z in (nz // 4, 3 * nz // 4, 0)]


def send_near(held):
    nz = lax.axis_size("z")
    step = nz // 8
    while step:
        held = held + lax.ppermute(held, "z", [(z, z + step) for z in range(0, nz, 2 * step)])
        step //= 2
    return held


def swapped(held):
    return lax.ppermute(held, "core", [(0, 1), (1, 0)])


def put_halves(core, mine, other, whole):
    half = mine.shape[0]
    whole[pl.ds(core * half, half), :] = mine[...]
    whole[pl.ds((1 - core) * half, half), :] = other[...]


def first_kernel(core_ref, slab, mine, other, out, whole):
    ncol, block = out.shape[:2]
    block -= SLICE
    put_halves(core_ref[0], mine, other, whole)
    right = split(whole[...])
    for i in range(ncol):
        out[i, :block, :] = product(split(slab[i * block : (i + 1) * block, :]), right, NN)


def cross_kernel(terms, rows, panel, other_av, out):
    ncol, block, nb = rows.shape
    cross = product(split(panel[...]), split(other_av[...]), TN)
    for i in range(ncol):
        cross = cross + product(split(rows[i]), split(terms[i, :block, :]), TN)
    out[:, block:, :] = cross.reshape(ncol, SLICE, nb)


def first(core, slab, rows, panel, other_av, mine, other):
    ncol, block, nb = rows.shape
    vmem = pl.BlockSpec(memory_space=pltpu.VMEM)
    shape = jax.ShapeDtypeStruct((ncol, block + SLICE, nb), F32)
    params = pltpu.CompilerParams(vmem_limit_bytes=VMEM)
    terms = pl.pallas_call(
        first_kernel,
        out_shape=shape,
        in_specs=[pl.BlockSpec(memory_space=pltpu.SMEM)] + [vmem] * 3,
        out_specs=vmem,
        scratch_shapes=[pltpu.VMEM((2 * block, nb), F32)],
        compiler_params=params,
        cost_estimate=pl.CostEstimate(
            flops=6*10**9, bytes_accessed=6 * slab.size, transcendentals=0
        ),
        name="first",
    )(core, slab, mine, other)
    return pl.pallas_call(
        cross_kernel,
        out_shape=shape,
        in_specs=[vmem] * 4,
        out_specs=vmem,
        input_output_aliases={0: 0},
        compiler_params=params,
        cost_estimate=pl.CostEstimate(
            flops=6 * rows.size * nb, bytes_accessed=8 * rows.size, transcendentals=0
        ),
        name="cross",
    )(terms, rows, panel, other_av)


def summed_kernel(terms, other_av, tfactor, wmat, part):
    block = wmat.shape[0]
    total = terms[0]
    for i in range(1, terms.shape[0]):
        total = total + terms[i]
    wmat[...] = exact(total[:block] + other_av[...], tfactor[...])
    part[...] = total[block:]


def summed(terms, other_av, tfactor):
    vmem = pl.BlockSpec(memory_space=pltpu.VMEM)
    return pl.pallas_call(
        summed_kernel,
        out_shape=(
            jax.ShapeDtypeStruct(other_av.shape, F32),
            jax.ShapeDtypeStruct((SLICE, other_av.shape[1]), F32),
        ),
        in_specs=[vmem] * 3,
        out_specs=(vmem, vmem),
        compiler_params=pltpu.CompilerParams(vmem_limit_bytes=VMEM),
        cost_estimate=pl.CostEstimate(
            flops=12 * other_av.size * tfactor.shape[0], bytes_accessed=4 * terms.size, transcendentals=0
        ),
        name="summed",
    )(terms, other_av, tfactor)


def spread_kernel(part, other, out):
    total = part[...] + other[...]
    for i in range(out.shape[0]):
        out[i] = total


def spread_sum(part, other):
    vmem = pl.BlockSpec(memory_space=pltpu.VMEM)
    return pl.pallas_call(
        spread_kernel,
        out_shape=jax.ShapeDtypeStruct((lax.axis_size("z"),) + part.shape, F32),
        in_specs=[vmem] * 2,
        out_specs=vmem,
        compiler_params=pltpu.CompilerParams(vmem_limit_bytes=VMEM),
        cost_estimate=pl.CostEstimate(flops=1*10**9, bytes_accessed=128 * part.size, transcendentals=0),
        name="spread",
    )(part, other)


def relayed_kernel(got, out):
    out[...] = got[...]


def relayed(got):
    vmem = pl.BlockSpec(memory_space=pltpu.VMEM)
    return pl.pallas_call(
        relayed_kernel,
        out_shape=jax.ShapeDtypeStruct(got.shape, F32),
        in_specs=[vmem],
        out_specs=vmem,
        compiler_params=pltpu.CompilerParams(vmem_limit_bytes=VMEM),
        cost_estimate=pl.CostEstimate(flops=60*10**9, bytes_accessed=8 * got.size, transcendentals=0),
        name="relayed",
    )(got)


def columns_kernel(core_ref, mine, other, wmine, wother, out):
    core, nb = core_ref[0], mine.shape[1]
    put_halves(core, wmine, wother, out.at[:, :nb])
    put_halves(core, mine, other, out.at[:, nb:])


def columns(core, *halves):
    half, nb = halves[0].shape
    vmem = pl.BlockSpec(memory_space=pltpu.VMEM)
    return pl.pallas_call(
        columns_kernel,
        out_shape=jax.ShapeDtypeStruct((2 * half, 2 * nb), F32),
        in_specs=[pl.BlockSpec(memory_space=pltpu.SMEM)] + [vmem] * 4,
        out_specs=vmem,
        compiler_params=pltpu.CompilerParams(vmem_limit_bytes=VMEM),
        cost_estimate=pl.CostEstimate(flops=6*10**9, bytes_accessed=32 * half * nb, transcendentals=0),
        name="columns",
    )(core, *halves)


def last_kernel(
    slab, rows, found, panel, wmat, tfactor, pair, updated, correction, result, loads, sems
):
    ncol, block, nb = rows.shape
    size = slab.shape[0] // PARTS
    copies = []
    for i in range(PARTS):
        here = pl.ds(i * size, size)
        copies.append(pltpu.make_async_copy(slab.at[here, :], result.at[here, :], loads.at[i]))
        copies[-1].start()
    factor = split(tfactor[...])
    inner = product(split(found[:, block:, :].reshape(nb, nb)), factor, NN)
    middle = product(factor, split(inner), TN)
    both = 0.5 * (middle + middle.T)
    right = pair[...]
    columns_v = right[:, nb:]
    turned = right[:, :nb] - product(split(columns_v), split(both), NN)
    right = split(jnp.concatenate([turned, columns_v], axis=1))
    step = ncol // PARTS
    stores = []
    for i in range(PARTS):
        here, part = pl.ds(i * size, size), slice(i * step, (i + 1) * step)
        left = jnp.concatenate(
            [rows[part].reshape(size, nb), found[part, :block, :].reshape(size, nb)], axis=1
        )
        change = product(split(left), right, NT)
        copies[i].wait()
        result[here, :] = result[here, :] - change
        stores.append(pltpu.make_async_copy(result.at[here, :], updated.at[here, :], sems.at[i]))
        stores[-1].start()
    correction[...] = wmat[...] - 0.5 * product(split(panel[...]), split(middle), NN)
    for store in stores:
        store.wait()


def last(slab, rows, found, panel, wmat, tfactor, pair):
    vmem = pl.BlockSpec(memory_space=pltpu.VMEM)
    return pl.pallas_call(
        last_kernel,
        out_shape=(
            jax.ShapeDtypeStruct(slab.shape, F32),
            jax.ShapeDtypeStruct(wmat.shape, F32),
        ),
        in_specs=[pl.BlockSpec(memory_space=pl.ANY)] + [vmem] * 6,
        out_specs=(pl.BlockSpec(memory_space=pl.ANY), vmem),
        scratch_shapes=[pltpu.VMEM(slab.shape, F32)] + [pltpu.SemaphoreType.DMA((PARTS,))] * 2,
        compiler_params=pltpu.CompilerParams(vmem_limit_bytes=LAST_VMEM),
        cost_estimate=pl.CostEstimate(
            flops=12 * slab.size * wmat.shape[1],
            bytes_accessed=4 * (2 * slab.size + 2 * rows.size),
            transcendentals=0,
        ),
        name="last",
    )(slab, rows, found, panel, wmat, tfactor, pair)


def on_device(slab, panel, tfactor, other_av):
    ncol = lax.axis_size(COL)
    block = panel.shape[0]
    core = lax.axis_index("core").astype(jnp.int32)[None]
    tied, spread = lax.optimization_barrier((panel, copies(panel, COL)))
    rows = lax.all_to_all(spread, COL, 0, 0)
    held = sum(place(tied, (12, 8, 4, 0)))
    mine = send_near(held)
    other = swapped(mine)
    sent = first(core, slab, rows, panel, other_av, mine, other)
    wmat, part = summed(lax.all_to_all(sent, COL, 0, 0), other_av, tfactor)
    other_part = swapped(part)
    early = relayed(sum(place(wmat, (12, 4, 0))))
    held = early + place(wmat, (8,))[0]
    part = lax.all_to_all(
        spread_sum(part, other_part), "z", 0, 0, axis_index_groups=[[(i + 8) % 16 for i in range(16)]]
    ).sum(axis=0)
    found = to_all(jnp.concatenate([wmat, part], axis=0), COL)
    wmine = send_near(held)
    pair = columns(core, mine, other, wmine, swapped(wmine))
    return last(slab, rows, found, panel, wmat, tfactor, pair)


def solution(mesh):
    nrow, ncol = mesh.devices.shape
    grid = Mesh(mesh.devices.reshape(nrow // 2, 2, 4, ncol // 4), ALL)
    placed = (P(ROW, COL), P(ALL, None), P(), P(ALL, None))
    return jax.shard_map(
        on_device,
        mesh=grid,
        in_specs=placed,
        out_specs=(P(ROW, COL), P(ALL, None)),
        check_vma=False,
    )
```
